32 devices in a mesh: seq: 4 (over z), tp: 8 (over y, x, core).
Axes of the slice: x: 2, y: 2, z: 4, core: 2. Of those that a mesh axis runs over, the one named last changes fastest.
Arguments:
- residual: bfloat16 [8192, 2048], P('seq', 'tp'), may hold values from -6 to 6
- attn_gain: bfloat16 [2048], replicated, may hold values from 0.25 to 1.75
- attn_in: bfloat16 [3, 2048, 2048], P(None, None, 'tp')
- attn_out: bfloat16 [2048, 2048], P('tp'), may hold values from -0.125 to 0.125
- ffn_gain: bfloat16 [2048], replicated, may hold values from 0.25 to 1.75
- ffn_in: bfloat16 [2, 2048, 20480], P(None, None, 'tp'), may hold values from -0.125 to 0.125
- ffn_out: bfloat16 [20480, 2048], P('tp'), may hold values from -0.0390625 to 0.0390625
- route_rows: int32 [4, 224], P('seq'), may hold values from 0 to 2047, as said below
- route_counts: int32 [4], replicated, may hold values from 1 to 224, 512 in all
Outputs:
- layer_out: bfloat16 [8192, 2048], P('seq', 'tp')
The draws below stay inside these ranges and needn't reach their ends.
Inputs may be any that keep to these rules, and one draw needn't show every extreme that they name: `route_rows`: in each row s the 224 entries are distinct positions of that shard; only the first route_counts[s] entries are used; each row holds 0 and 2047. `route_counts`: the counts sum to 512 and the largest is exactly 224.
All inputs are finite; a program needn't handle non-finite values.
Results may differ from the reference program's by a relative error of at most 0.014.
Values may be sent and summed in bfloat16 or wider, within the bound.
No kernel may reach another device: no remote copies, remote signals or barrier semaphores. Data moves between devices by JAX's collectives and lax.ppermute only.
A program may use at most 128 MiB of HBM per device.

```python
import math
import jax
import jax.numpy as jnp
import numpy as np
from jax import lax

D = 2048
HEADS = 32
HD = 64
FF = 20480
TOK_SEQ = 2048
RADIUS = 127
TOKENS = 8192
ROUTED = 512
CAP = 224
N_SEQ = 4
N_TP = 8


def draw_attn_in(key, part):
    key_list = jax.random.split(jax.random.fold_in(key, 11), 1)
    base_draw = jax.random.normal(key_list[0], (3, D, D), jnp.float32) / D ** 0.5
    return base_draw.astype(jnp.bfloat16)


def draw_route_rows(key, part):

    def one_shard(shard_key):
        first_key, second_key = jax.random.split(shard_key)
        middle = jax.random.permutation(first_key, TOK_SEQ - 2)[:CAP - 2].astype(jnp.int32) + 1
        picked = jnp.concatenate([jnp.array([0, TOK_SEQ - 1], jnp.int32), middle])
        return jax.random.permutation(second_key, picked)
    return jax.vmap(one_shard)(jax.random.split(jax.random.fold_in(key, 23), N_SEQ))


def shard_levels(stream_key, shape, cuts, least, top_value):
    gain, own = 1.0, jax.random.fold_in(stream_key, 6)
    for dim, blocks in cuts:
        draws = jnp.exp(jax.random.uniform(jax.random.fold_in(own, dim), (blocks,), jnp.float32, least / len(cuts), top_value / len(cuts)))
        gain = gain * jnp.repeat(draws, shape[dim] // blocks).reshape([-1 if axis == dim else 1 for axis in range(len(shape))])
    return gain


def split_up(count, total, bound, lean):
    loads = [(1 << 20) // math.isqrt(rank ** lean) + 1 for rank in range(2, count + 1)]
    rest, given = total - bound - (count - 1), [1] * (count - 1)
    while rest > 0:
        free = [i for i in range(count - 1) if given[i] < bound]
        whole, left = sum([loads[i] for i in free]), rest
        for i in free:
            more = min(bound - given[i], max(1, left * loads[i] // whole), rest)
            given[i] = given[i] + more
            rest = rest - more
    return np.array([bound] + given)


def ragged_sizes(own_key, amount, total, limit, skew):
    if amount == 2:
        one = jax.random.randint(own_key, (), max(1, total - limit), min(limit, total - 1) + 1)
        return jnp.stack([one, total - one])
    tallies = jnp.asarray(split_up(amount, total, limit, skew), jnp.int32)
    pairs = (amount - 1) // 2
    source_of, sink = tallies[1:1 + 2 * pairs:2], tallies[2:2 + 2 * pairs:2]
    margin = jnp.minimum(source_of - 1, limit - sink)
    shifted = jax.random.randint(jax.random.fold_in(own_key, 1), (pairs,), 0, 1 << 20) % (margin + 1)
    tallies = tallies.at[1:1 + 2 * pairs:2].set(source_of - shifted).at[2:2 + 2 * pairs:2].set(sink + shifted)
    return tallies[jax.random.permutation(jax.random.fold_in(own_key, 2), amount)]


def centred(stream_key, shape, spread, reach, shards=(), held_as=jnp.bfloat16):
    drawn = jax.random.normal(stream_key, shape, jnp.float32) * spread
    if len(shards) > 0:
        drawn = shard_levels(stream_key, shape, shards, -0.22, 0.18) * drawn
    return jnp.clip(drawn, min=-reach, max=reach).astype(held_as)


def setup_inputs(seed: int = 0) -> dict:
    seeds = jax.random.split(jax.random.key(seed), 10)
    residual = centred(seeds[0], (TOKENS, D), 1.0, 6.0, ((0, 4), (1, 8)))
    attn_gain = jnp.clip(1.0 + 0.15 * jax.random.normal(seeds[1], (D,), jnp.float32), 0.25, 1.75).astype(jnp.bfloat16)
    attn_in = draw_attn_in(jax.random.fold_in(seeds[9], 71), 0)
    attn_out = centred(seeds[3], (D, D), D ** -0.5, 0.125, ((0, 8),))
    ffn_gain = jnp.clip(1.0 + 0.15 * jax.random.normal(seeds[4], (D,), jnp.float32), 0.25, 1.75).astype(jnp.bfloat16)
    ffn_in = centred(seeds[5], (2, D, FF), D ** -0.5, 0.125, ((2, 8),))
    ffn_out = centred(seeds[6], (FF, D), FF ** -0.5, 0.0390625, ((0, 8),))
    route_rows = draw_route_rows(jax.random.fold_in(seeds[9], 71), 0)
    route_counts = ragged_sizes(seeds[8], N_SEQ, ROUTED, CAP, 2).astype(jnp.int32)
    return {"residual": residual, "attn_gain": attn_gain, "attn_in": attn_in, "attn_out": attn_out, "ffn_gain": ffn_gain, "ffn_in": ffn_in, "ffn_out": ffn_out, "route_rows": route_rows, "route_counts": route_counts}


epsilon = 1e-06

def rms_norm(values, gain_row):
    wide = values.astype(jnp.float32)
    mean_square = lax.optimization_barrier(jnp.mean(wide * wide, axis=-1, keepdims=True))
    return (wide * lax.rsqrt(mean_square + epsilon) * gain_row.astype(jnp.float32)).astype(jnp.bfloat16)

def reference(residual, attn_gain, attn_in, attn_out, ffn_gain, ffn_in, ffn_out, route_rows, route_counts):
    length = TOKENS
    block = min(512, TOK_SEQ)
    span = block + 2 * RADIUS
    normed = rms_norm(residual, attn_gain)
    query_rows = jnp.dot(normed, attn_in[0], preferred_element_type=jnp.float32).astype(jnp.bfloat16).reshape(length, HEADS, HD)
    key_rows = jnp.dot(normed, attn_in[1], preferred_element_type=jnp.float32).astype(jnp.bfloat16).reshape(length, HEADS, HD)
    value_rows = jnp.dot(normed, attn_in[2], preferred_element_type=jnp.float32).astype(jnp.bfloat16).reshape(length, HEADS, HD)
    padded_keys = jnp.pad(key_rows, ((RADIUS, RADIUS), (0, 0), (0, 0)))
    padded_values = jnp.pad(value_rows, ((RADIUS, RADIUS), (0, 0), (0, 0)))

    def attend(block_id):
        start = block_id * block
        query_blk = lax.dynamic_slice_in_dim(query_rows, start, block, 0).astype(jnp.float32)
        key_blk = lax.dynamic_slice_in_dim(padded_keys, start, span, 0).astype(jnp.float32)
        value_blk = lax.dynamic_slice_in_dim(padded_values, start, span, 0).astype(jnp.float32)
        query_pos = start + jnp.arange(block, dtype=jnp.int32)
        key_pos = start - RADIUS + jnp.arange(span, dtype=jnp.int32)
        usable = (jnp.abs(query_pos[:, None] - key_pos[None, :]) <= RADIUS) & (key_pos[None, :] >= 0) & (key_pos[None, :] < length)
        scores = jnp.einsum('qhd,khd->hqk', query_blk, key_blk) / HD ** 0.5
        scores = jnp.where(usable[None], scores, -jnp.inf)
        top = lax.optimization_barrier(jnp.max(scores, axis=-1, keepdims=True))
        expo = jnp.exp(scores - top)
        prob_rows = (expo / lax.optimization_barrier(jnp.sum(expo, axis=-1, keepdims=True))).astype(jnp.bfloat16)
        context = jnp.einsum('hqk,khd->qhd', prob_rows.astype(jnp.float32), value_blk)
        return context.astype(jnp.bfloat16).reshape(block, D)
    context = lax.map(attend, jnp.arange(length // block, dtype=jnp.int32)).reshape(length, D)
    mixed = jnp.dot(context, attn_out, preferred_element_type=jnp.float32)
    updated = (residual.astype(jnp.float32) + mixed).astype(jnp.bfloat16)
    owned = updated.reshape(N_SEQ, TOK_SEQ, D)
    picked = jax.vmap(lambda rows_all, index_row: jnp.take(rows_all, index_row, axis=0))(owned, route_rows)
    picked = picked.reshape(N_SEQ * CAP, D)
    normed_rows = rms_norm(picked, ffn_gain)
    gate_part = jnp.dot(normed_rows, ffn_in[0], preferred_element_type=jnp.float32)
    up_part = jnp.dot(normed_rows, ffn_in[1], preferred_element_type=jnp.float32)
    hidden = (jax.nn.gelu(gate_part, approximate=True) * up_part).astype(jnp.bfloat16)
    width = FF // N_TP

    def add_group(group, total):
        start = jnp.asarray(group, jnp.int32) * width
        part_hidden = lax.dynamic_slice_in_dim(hidden, start, width, 1)
        part_weight = lax.dynamic_slice_in_dim(ffn_out, start, width, 0)
        term = jnp.dot(part_hidden, part_weight, preferred_element_type=jnp.float32).astype(jnp.bfloat16)
        term = lax.optimization_barrier(term)
        return total + term.astype(jnp.float32)
    heavy = lax.fori_loop(0, N_TP, add_group, jnp.zeros((N_SEQ * CAP, D), jnp.float32))
    slots = jnp.arange(CAP, dtype=jnp.int32)
    usable_slots = slots[None, :] < route_counts[:, None]
    heavy = jnp.where(usable_slots[:, :, None], heavy.reshape(N_SEQ, CAP, D), 0.0)
    result = jax.vmap(lambda rows_all, index_row, extra: rows_all.at[index_row].add(extra))(owned.astype(jnp.float32), route_rows, heavy)
    return result.reshape(TOKENS, D).astype(jnp.bfloat16)
```

```python
import functools

import jax
import jax.numpy as jnp
from jax import lax
from jax.experimental import pallas as pl
from jax.experimental.pallas import tpu as pltpu
from jax.sharding import PartitionSpec as P

HD = 64
RADIUS = 127
BLK = 128
VMEM_LIMIT = 56 * 1024 * 1024

epsilon = 1e-06
f32 = jnp.float32
bf16 = jnp.bfloat16

VMEM = pl.BlockSpec(memory_space=pltpu.VMEM)
SMEM = pl.BlockSpec(memory_space=pltpu.SMEM)


def params():
    return pltpu.CompilerParams(vmem_limit_bytes=VMEM_LIMIT)


class Pairs:
    def __init__(self):
        self.core = [(i, i ^ 1) for i in range(8)]
        self.first = [(i, i ^ (4 if i & 1 else 2)) for i in range(8)]
        self.second = [(i, i ^ (2 if i & 1 else 4)) for i in range(8)]

    def offsets(self, width):
        me = lax.axis_index("tp")
        first = jnp.where(me & 1 == 1, 4, 2)
        second = 6 - first
        blocks = [0, first, second, 6, 1, 1 ^ second, 1 ^ first, 7]
        return jnp.stack([(me ^ block) * width for block in blocks]).astype(jnp.int32)


def move(value, pairs):
    return lax.ppermute(value, "tp", pairs)


def gather_blocks(pairs, own):
    first = move(own, pairs.first)
    second = move(own, pairs.second)
    across = move(first, pairs.second)
    same_chip = [own, first, second, across]
    return same_chip + [move(block, pairs.core) for block in same_chip]


def add(left, right):
    return left.astype(f32) + right.astype(f32)


def reduce_blocks(pairs, keep, send):
    other = move(send, pairs.core)
    across = move(add(keep[3], other[3]).astype(bf16), pairs.first)
    near = move(add(keep[1], other[1]).astype(bf16), pairs.first)
    turned = (add(keep[2], other[2]) + across.astype(f32)).astype(bf16)
    far = move(turned, pairs.second)
    return add(keep[0], other[0]) + near.astype(f32) + far.astype(f32)


def put_normed(blocks, offsets, gain_ref, normed):
    total = None
    for block in blocks:
        wide = block[...].astype(f32)
        total = wide * wide if total is None else total + wide * wide
    width = blocks[0].shape[1]
    features = width * len(blocks)
    scale = lax.rsqrt(jnp.sum(total, axis=-1, keepdims=True) / features + epsilon)
    for number, block in enumerate(blocks):
        if len(blocks) == 1:
            columns = slice(None)
        else:
            columns = pl.ds(pl.multiple_of(offsets[number], width), width)
        gained = block[...].astype(f32) * scale * gain_ref[:, columns].astype(f32)
        normed[:, columns] = gained.astype(bf16)


def qkv_kernel(count, offsets, gain_ref, weight_ref, *refs):
    blocks, outs, normed = refs[:count], refs[count : count + 3], refs[count + 3]
    put_normed(blocks, offsets, gain_ref, normed)
    for number, out in enumerate(outs):
        value = jnp.dot(normed[...], weight_ref[number], preferred_element_type=f32)
        if number == 0:
            value = value * (1.0 / HD**0.5)
        out[...] = value.astype(bf16)


def qkv(blocks, offsets, gain_row, attn_in):
    rows, width = blocks[0].shape
    features, local_width = attn_in.shape[1:]
    count = len(blocks)
    tile = rows // 2 if rows >= 512 else rows
    out = jax.ShapeDtypeStruct((rows, local_width), bf16)
    return pl.pallas_call(
        functools.partial(qkv_kernel, count),
        grid=(rows // tile,),
        out_shape=[out] * 3,
        in_specs=[
            SMEM,
            pl.BlockSpec((1, features), lambda i: (0, 0)),
            pl.BlockSpec((3, features, local_width), lambda i: (0, 0, 0)),
        ]
        + [pl.BlockSpec((tile, width), lambda i: (i, 0))] * count,
        out_specs=[pl.BlockSpec((tile, local_width), lambda i: (i, 0))] * 3,
        scratch_shapes=[pltpu.VMEM((tile, features), bf16)],
        compiler_params=params(),
        cost_estimate=pl.CostEstimate(
            flops=2 * rows * features * 3 * local_width,
            bytes_accessed=2 * (rows * features + 3 * features * local_width + 3 * rows * local_width),
            transcendentals=0,
        ),
        name="norm_qkv",
    )(offsets, gain_row, attn_in, *blocks)


def project(rows_ref, weight_ref, offsets, outs):
    if len(outs) == 1:
        outs[0][...] = jnp.dot(rows_ref[...], weight_ref[...], preferred_element_type=f32).astype(bf16)
        return
    width = outs[0].shape[2]
    for side, out in enumerate(outs):
        for number in range(4):
            columns = pl.ds(pl.multiple_of(offsets[4 * side + number], width), width)
            value = jnp.dot(rows_ref[...], weight_ref[:, columns], preferred_element_type=f32)
            out[number] = value.astype(bf16)


def partial_shapes(split, rows, features, width):
    if split:
        return [jax.ShapeDtypeStruct((4, rows, width), bf16)] * 2
    return [jax.ShapeDtypeStruct((rows, features), bf16)]


def attention_kernel(queries, keys, n_arrays, n_outs, ends, offsets, weight_ref, *refs):
    arrays, outs, context = refs[:n_arrays], refs[n_arrays : n_arrays + n_outs], refs[-1]
    width = weight_ref.shape[0]
    heads = width // HD
    span = 3 * BLK
    row = lax.broadcasted_iota(jnp.int32, (BLK, span), 0)
    column = lax.broadcasted_iota(jnp.int32, (BLK, span), 1)
    band = (column - row >= BLK - RADIUS) & (column - row <= BLK + RADIUS)
    head_of = lax.broadcasted_iota(jnp.int32, (BLK, width), 1) // HD

    def load(kind, block):
        number, start = keys[block]
        return arrays[3 * number + kind][start : start + BLK, :]

    for place, block in enumerate(queries):
        query = load(0, block)
        stacked = jnp.concatenate(
            [jnp.where(head_of == head, query, jnp.zeros_like(query)) for head in range(heads)], axis=0
        )
        key = jnp.concatenate([load(1, block + step) for step in (-1, 0, 1)], axis=0)
        value = jnp.concatenate([load(2, block + step) for step in (-1, 0, 1)], axis=0)
        scores = lax.dot_general(stacked, key, (((1,), (1,)), ((), ())), preferred_element_type=f32)
        usable = band
        if keys[block - 1] is keys["low"]:
            usable = usable & ((column >= BLK) | (ends[0] > 0))
        if keys[block + 1] is keys["high"]:
            usable = usable & ((column < 2 * BLK) | (ends[1] > 0))
        scores = jnp.where(usable[None], scores.reshape(heads, BLK, span), -jnp.inf)
        top = jnp.max(scores, axis=-1, keepdims=True)
        expo = jnp.exp(scores - top)
        share = 1.0 / jnp.sum(expo, axis=-1, keepdims=True)
        expo = expo.astype(bf16).reshape(heads * BLK, span)
        mixed = jnp.dot(expo, value, preferred_element_type=f32).reshape(heads, BLK, width) * share
        chosen = mixed[0]
        for head in range(1, heads):
            chosen = jnp.where(head_of == head, mixed[head], chosen)
        context[place * BLK : (place + 1) * BLK, :] = chosen.astype(bf16)
    project(context, weight_ref, offsets, outs)


def attention(queries, keys, arrays, ends, offsets, attn_out, split):
    rows = len(queries) * BLK
    width, features = attn_out.shape
    flat = [piece for triple in arrays for piece in triple]
    outs = partial_shapes(split, rows, features, width)
    heads = width // HD
    return pl.pallas_call(
        functools.partial(attention_kernel, queries, keys, len(flat), len(outs)),
        out_shape=outs,
        in_specs=[SMEM, SMEM, VMEM] + [VMEM] * len(flat),
        out_specs=[VMEM] * len(outs),
        scratch_shapes=[pltpu.VMEM((rows, width), bf16)],
        compiler_params=params(),
        cost_estimate=pl.CostEstimate(
            flops=2 * rows * (2 * 3 * BLK * width * heads + width * features),
            bytes_accessed=2 * (rows * features + width * features + 6 * rows * width),
            transcendentals=rows * heads * 3 * BLK,
        ),
        name="band_attention",
    )(ends, offsets, attn_out, *flat)


def ffn_kernel(count, n_outs, steps, offsets, gain_ref, in_ref, out_weight_ref, *refs):
    blocks, outs = refs[:count], refs[count : count + n_outs]
    normed, total = refs[count + n_outs :]
    step = pl.program_id(0)

    @pl.when(step == 0)
    def start():
        put_normed(blocks, offsets, gain_ref, normed)
        total[...] = jnp.zeros_like(total)

    gate = jnp.dot(normed[...], in_ref[0], preferred_element_type=f32)
    up = jnp.dot(normed[...], in_ref[1], preferred_element_type=f32)
    hidden = (jax.nn.gelu(gate, approximate=True) * up).astype(bf16)
    total[...] += jnp.dot(hidden, out_weight_ref[...], preferred_element_type=f32)

    @pl.when(step == steps - 1)
    def finish():
        if n_outs == 1:
            outs[0][...] = total[...].astype(bf16)
        else:
            width = outs[0].shape[2]
            for side, out in enumerate(outs):
                for number in range(4):
                    columns = pl.ds(pl.multiple_of(offsets[4 * side + number], width), width)
                    out[number] = total[:, columns].astype(bf16)


def ffn(blocks, offsets, gain_row, ffn_in, ffn_out, split):
    rows, width = blocks[0].shape
    hidden, features = ffn_out.shape
    count = len(blocks)
    tile = 256 if hidden % 256 == 0 else 128
    steps = hidden // tile
    outs = partial_shapes(split, rows, features, width)
    return pl.pallas_call(
        functools.partial(ffn_kernel, count, len(outs), steps),
        grid=(steps,),
        out_shape=outs,
        in_specs=[
            SMEM,
            pl.BlockSpec((1, features), lambda i: (0, 0)),
            pl.BlockSpec((2, features, tile), lambda i: (0, 0, i)),
            pl.BlockSpec((tile, features), lambda i: (i, 0)),
        ]
        + [pl.BlockSpec((rows, width), lambda i: (0, 0))] * count,
        out_specs=[pl.BlockSpec(out.shape, lambda i, dims=len(out.shape): (0,) * dims) for out in outs],
        scratch_shapes=[pltpu.VMEM((rows, features), bf16), pltpu.VMEM((rows, features), f32)],
        compiler_params=params(),
        cost_estimate=pl.CostEstimate(
            flops=2 * rows * features * 3 * hidden,
            bytes_accessed=2 * 3 * hidden * features,
            transcendentals=rows * hidden,
        ),
        name="heavy_ffn",
    )(offsets, gain_row, ffn_in, ffn_out, *blocks)


def spread_kernel(tile, updated_ref, heavy_ref, rows_ref, used_ref, out_ref):
    slots = heavy_ref.shape[0]
    heavy = jnp.where(used_ref[...] > 0, heavy_ref[...], 0.0)
    coarse = heavy.astype(bf16)
    fine = (heavy - coarse.astype(f32)).astype(bf16)
    position = lax.broadcasted_iota(jnp.int32, (tile, slots), 0) + pl.program_id(0) * tile
    one_hot = (position == rows_ref[...]).astype(f32).astype(bf16)
    extra = jnp.dot(one_hot, coarse, preferred_element_type=f32)
    extra += jnp.dot(one_hot, fine, preferred_element_type=f32)
    out_ref[...] = (updated_ref[...].astype(f32) + extra).astype(bf16)


def spread(updated, heavy, route_rows, usable_slots):
    rows, width = updated.shape
    slots = heavy.shape[0]
    tile = min(512, rows)
    return pl.pallas_call(
        functools.partial(spread_kernel, tile),
        grid=(rows // tile,),
        out_shape=jax.ShapeDtypeStruct((rows, width), bf16),
        in_specs=[
            pl.BlockSpec((tile, width), lambda i: (i, 0)),
            pl.BlockSpec((slots, width), lambda i: (0, 0)),
            pl.BlockSpec((1, slots), lambda i: (0, 0)),
            pl.BlockSpec((slots, 1), lambda i: (0, 0)),
        ],
        out_specs=pl.BlockSpec((tile, width), lambda i: (i, 0)),
        compiler_params=params(),
        name="spread_rows",
    )(updated, heavy, route_rows, usable_slots.astype(jnp.int32)[:, None])


def plan(total):
    middle = max(2, (total - 4) // 6)
    left = (total - 4 - middle) // 2
    cut, end = 2 + left, total - 2
    chunks = [
        [0, 1, end, end + 1],
        list(range(2, cut)),
        list(range(cut + middle, end)),
        list(range(cut, cut + middle)),
    ]
    groups = [
        None,
        list(range(0, cut - 1)),
        list(range(cut + middle + 1, total)),
        list(range(cut - 1, cut + middle + 1)),
    ]
    return chunks, groups


def local(
    residual, attn_gain, attn_in, attn_out, ffn_gain, ffn_in, ffn_out, route_rows, route_counts
):
    seq_count = lax.axis_size("seq")
    seq_index = lax.axis_index("seq")
    tok_rows, width = residual.shape
    split = lax.axis_size("tp") == 8
    if split:
        pairs = Pairs()
        offsets = pairs.offsets(width)
        gather = functools.partial(gather_blocks, pairs)
        reduce = functools.partial(reduce_blocks, pairs)
    else:
        offsets = jnp.zeros((1,), jnp.int32)
        gather = lambda own: [lax.all_gather(own, "tp", axis=1, tiled=True)]
        reduce = lambda part: lax.psum_scatter(part, "tp", scatter_dimension=1, tiled=True).astype(f32)

    chunks, groups = plan(tok_rows // BLK)
    ends = jnp.stack([seq_index > 0, seq_index < seq_count - 1]).astype(jnp.int32)

    def rows_of(array, blocks):
        pieces, start = [], 0
        for at in range(1, len(blocks) + 1):
            if at == len(blocks) or blocks[at] != blocks[at - 1] + 1:
                pieces.append(array[blocks[start] * BLK : (blocks[at - 1] + 1) * BLK])
                start = at
        return pieces[0] if len(pieces) == 1 else jnp.concatenate(pieces, axis=0)

    keys, arrays, pending, updated = {}, [], [], [None] * len(chunks)
    held = []
    for number, (blocks, queries) in enumerate(zip(chunks, groups)):
        own = rows_of(residual, blocks)
        if number >= 2:
            own, _ = lax.optimization_barrier((own, held[number - 2]))
        whole = gather(own)
        held.append(whole[1] if split else whole[0])
        triple = qkv(whole, offsets, attn_gain[None], attn_in)
        for at, block in enumerate(blocks):
            keys[block] = (len(arrays), at * BLK)
        arrays.append(triple)
        if number == 0:
            up = [(i, i + 1) for i in range(seq_count - 1)]
            down = [(target, source) for source, target in up]
            low = [lax.ppermute(kind[-BLK:], "seq", up) for kind in triple[1:]]
            high = [lax.ppermute(kind[:BLK], "seq", down) for kind in triple[1:]]
            keys["low"] = keys[-1] = (len(arrays), 0)
            keys["high"] = keys[blocks[-1] + 1] = (len(arrays) + 1, 0)
            arrays.append([low[0]] + low)
            arrays.append([high[0]] + high)
        if queries is None:
            continue
        needed = sorted({keys[b + step][0] for b in queries for step in (-1, 0, 1)})
        place = {array: at for at, array in enumerate(needed)}
        inner = {name: (place.get(array), start) for name, (array, start) in keys.items()}
        inner["low"] = inner[-1]
        inner["high"] = inner[chunks[0][-1] + 1]
        parts = attention(
            queries, inner, [arrays[array] for array in needed], ends, offsets, attn_out, split
        )
        mixed = reduce(*parts)
        pending.append((queries[0], (add(rows_of(residual, queries), mixed)).astype(bf16)))
    updated = jnp.concatenate([rows for _, rows in sorted(pending, key=lambda pair: pair[0])], axis=0)

    slots = jnp.arange(route_rows.shape[1], dtype=jnp.int32)
    row_count = lax.dynamic_index_in_dim(route_counts, seq_index, 0, keepdims=False)
    taken = jnp.take(updated, route_rows[0], axis=0)
    heavy = reduce(*ffn(gather(taken), offsets, ffn_gain[None], ffn_in, ffn_out, split))
    return spread(updated, heavy, route_rows, slots < row_count)


def solution(mesh):
    in_specs = (
        P("seq", "tp"),
        P(),
        P(None, None, "tp"),
        P("tp", None),
        P(),
        P(None, None, "tp"),
        P("tp", None),
        P("seq", None),
        P(),
    )
    out_specs = P("seq", "tp")
    return jax.shard_map(local, mesh=mesh, in_specs=in_specs, out_specs=out_specs, check_vma=False)
```

```python
import functools

import jax
import jax.numpy as jnp
from jax import lax
from jax.experimental import pallas as pl
from jax.experimental.pallas import tpu as pltpu
from jax.sharding import PartitionSpec as P

HD = 64
RADIUS = 127
BLK = 128

epsilon = 1e-06
f32 = jnp.float32
bf16 = jnp.bfloat16

VMEM = pl.BlockSpec(memory_space=pltpu.VMEM)
SMEM = pl.BlockSpec(memory_space=pltpu.SMEM)
ANY = pl.BlockSpec(memory_space=pl.ANY)


def cost(flops):
    return pl.CostEstimate(flops=2 * flops, bytes_accessed=1, transcendentals=0)


def params(mebibytes):
    return pltpu.CompilerParams(vmem_limit_bytes=mebibytes * 1024 * 1024)


class Pairs:
    def __init__(self):
        self.core = [(i, i ^ 1) for i in range(8)]
        self.first = [(i, i ^ (4 if i & 1 else 2)) for i in range(8)]
        self.second = [(i, i ^ (2 if i & 1 else 4)) for i in range(8)]

    def places(self, width):
        offsets = self.offsets(width)
        return jnp.concatenate([offsets, offsets[:3], offsets[6:7], offsets[3:6], offsets[7:]])

    def offsets(self, width):
        me = lax.axis_index("tp")
        first = jnp.where(me & 1 == 1, 4, 2)
        second = 6 - first
        blocks = [0, first, second, 1, 1 ^ second, 1 ^ first, 6, 7]
        return jnp.stack([(me ^ block) * width for block in blocks]).astype(jnp.int32)


def move(value, pairs):
    return lax.ppermute(value, "tp", pairs)


def gather_blocks(pairs, own, chunks):
    first = move(own, pairs.first)
    second = move(own, pairs.second)
    same_chip = [own, first, second]
    whole = same_chip + [move(block, pairs.core) for block in same_chip]
    across = [move(rows_of(first, chunk), pairs.second) for chunk in chunks]
    return whole, [[block, move(block, pairs.core)] for block in across]


def gather_few(pairs, own):
    first = move(own, pairs.first)
    second = move(own, pairs.second)
    across = move(first, pairs.second)
    same_chip = [own, first, second, across]
    cores = [move(block, pairs.core) for block in same_chip]
    return same_chip[:3] + cores[:3] + [across, cores[3]]


def rows_of(array, blocks):
    pieces = [array[start : start + rows] for start, rows, _ in runs_of(blocks)]
    return pieces[0] if len(pieces) == 1 else jnp.concatenate(pieces, axis=0)


def runs_of(blocks):
    runs, start = [], 0
    for at in range(1, len(blocks) + 1):
        if at == len(blocks) or blocks[at] != blocks[at - 1] + 1:
            runs.append((blocks[start] * BLK, (at - start) * BLK, start * BLK))
            start = at
    return runs


def add(left, right):
    return left.astype(f32) + right.astype(f32)


def reduce_blocks(pairs, keep, send):
    other = move(send, pairs.core)
    across = move(add(keep[3], other[3]).astype(bf16), pairs.first)
    near = move(add(keep[1], other[1]).astype(bf16), pairs.first)
    turned = (add(keep[2], other[2]) + across.astype(f32)).astype(bf16)
    far = move(turned, pairs.second)
    return [keep, other, near, far], [other, across, far]


def total(terms):
    wide = [(term[0] if term.ndim == 3 else term).astype(f32) for term in terms]
    return functools.reduce(lambda left, right: left + right, wide)


def row_scale(blocks, features):
    total = None
    for block in blocks:
        wide = block.astype(f32)
        total = wide * wide if total is None else total + wide * wide
    return lax.rsqrt(jnp.sum(total, axis=-1, keepdims=True) / features + epsilon)


def columns_of(count, width, offsets, number):
    if count == 1:
        return slice(None)
    return pl.ds(pl.multiple_of(offsets[number], width), width)


def qkv_kernel(count, runs, offsets, gain_ref, weight_ref, *refs):
    blocks, (query_ref, pair_ref, gained) = refs[:count], refs[-3:]
    rows, features = gained.shape
    width = blocks[0].shape[1]
    scales = []
    for first, amount, place in runs:
        values = []
        for block in blocks:
            start = place if block.shape[0] == rows else first
            values.append(block[start : start + amount, :])
        for number, value in enumerate(values):
            columns = columns_of(count, width, offsets, number)
            gained[place : place + amount, columns] = value * (gain_ref[:, columns] * 0.0625)
        scales.append(row_scale(values, features) * 16.0)
    scale = scales[0] if len(scales) == 1 else jnp.concatenate(scales, axis=0)
    query = jnp.dot(gained[...], weight_ref[0], preferred_element_type=f32)
    query_ref[...] = (query * (scale * (1.0 / HD**0.5))).astype(bf16)
    local_width = query_ref.shape[1]
    for number in range(2):
        value = jnp.dot(gained[...], weight_ref[1 + number], preferred_element_type=f32)
        pair_ref[:, number * local_width : (number + 1) * local_width] = (value * scale).astype(bf16)


def qkv(blocks, runs, offsets, gain_row, attn_in, after):
    rows = sum(amount for _, amount, _ in runs)
    features, local_width = attn_in.shape[1:]
    count = len(blocks)
    return pl.pallas_call(
        functools.partial(qkv_kernel, count, runs),
        out_shape=[
            jax.ShapeDtypeStruct((rows, local_width), bf16),
            jax.ShapeDtypeStruct((rows, 2 * local_width), bf16),
        ],
        in_specs=[SMEM, VMEM, VMEM] + [VMEM] * count + [ANY] * len(after),
        out_specs=[VMEM] * 2,
        scratch_shapes=[pltpu.VMEM((rows, features), bf16)],
        compiler_params=params(12),
        cost_estimate=cost(2 * rows * features * 3 * local_width),
        name="norm_qkv",
    )(offsets, gain_row, attn_in, *blocks, *after)


def project(rows_ref, weight_ref, offsets, outs):
    if len(outs) == 1:
        outs[0][...] = jnp.dot(rows_ref[...], weight_ref[...], preferred_element_type=f32).astype(bf16)
        return
    width = outs[0].shape[2]
    for side, out in enumerate(outs):
        for number in range(4):
            columns = pl.ds(pl.multiple_of(offsets[8 + 4 * side + number], width), width)
            value = jnp.dot(rows_ref[...], weight_ref[:, columns], preferred_element_type=f32)
            out[number] = value.astype(bf16)


def partial_shapes(split, rows, features, width):
    if split:
        return [jax.ShapeDtypeStruct((4, rows, width), bf16)] * 2
    return [jax.ShapeDtypeStruct((rows, features), bf16)]


def stack_heads(query, head_of, heads):
    return jnp.concatenate(
        [jnp.where(head_of == head, query, jnp.zeros_like(query)) for head in range(heads)], axis=0
    )


def pick_heads(mixed, head_of):
    chosen = mixed[0]
    for head in range(1, mixed.shape[0]):
        chosen = jnp.where(head_of == head, mixed[head], chosen)
    return chosen.astype(bf16)


def attention_kernel(queries, keys, n_arrays, n_outs, ends, offsets, weight_ref, *refs):
    arrays, outs, context = refs[:n_arrays], refs[-1 - n_outs : -1], refs[-1]
    width = weight_ref.shape[0]
    heads = width // HD
    span = 3 * BLK
    row = lax.broadcasted_iota(jnp.int32, (BLK, span), 0)
    column = lax.broadcasted_iota(jnp.int32, (BLK, span), 1)
    band = (column - row >= BLK - RADIUS) & (column - row <= BLK + RADIUS)
    head_of = lax.broadcasted_iota(jnp.int32, (BLK, width), 1) // HD

    def load(kind, block):
        number, start = keys[block]
        if kind == 0:
            return arrays[2 * number][start : start + BLK, :]
        return arrays[2 * number + 1][start : start + BLK, (kind - 1) * width : kind * width]

    for place, block in enumerate(queries):
        stacked = stack_heads(load(0, block), head_of, heads)
        key = jnp.concatenate([load(1, block + step) for step in (-1, 0, 1)], axis=0)
        value = jnp.concatenate([load(2, block + step) for step in (-1, 0, 1)], axis=0)
        scores = lax.dot_general(stacked, key, (((1,), (1,)), ((), ())), preferred_element_type=f32)
        usable = band
        if keys[block - 1] is keys["low"]:
            usable = usable & ((column >= BLK) | (ends[0] > 0))
        if keys[block + 1] is keys["high"]:
            usable = usable & ((column < 2 * BLK) | (ends[1] > 0))
        scores = jnp.where(usable[None], scores.reshape(heads, BLK, span), -jnp.inf)
        top = jnp.max(scores, axis=-1, keepdims=True)
        expo = jnp.exp(scores - top)
        share = 1.0 / jnp.sum(expo, axis=-1, keepdims=True)
        expo = expo.astype(bf16).reshape(heads * BLK, span)
        mixed = jnp.dot(expo, value, preferred_element_type=f32).reshape(heads, BLK, width) * share
        context[place * BLK : (place + 1) * BLK, :] = pick_heads(mixed, head_of)
    project(context, weight_ref, offsets, outs)


def attention(queries, keys, arrays, ends, offsets, attn_out, split, after):
    rows = len(queries) * BLK
    width, features = attn_out.shape
    flat = [piece for pair in arrays for piece in pair]
    outs = partial_shapes(split, rows, features, width)
    heads = width // HD
    return pl.pallas_call(
        functools.partial(attention_kernel, queries, keys, len(flat), len(outs)),
        out_shape=outs,
        in_specs=[SMEM, SMEM, VMEM] + [VMEM] * len(flat) + [ANY] * len(after),
        out_specs=[VMEM] * len(outs),
        scratch_shapes=[pltpu.VMEM((rows, width), bf16)],
        compiler_params=params(12),
        cost_estimate=cost(2 * rows * (2 * 3 * BLK * width * heads + width * features)),
        name="band_attention",
    )(ends, offsets, attn_out, *flat, *after)


def routed_kernel(places, n_outs, origin, ends, offsets, rows_ref, weight_ref, *refs):
    count = len(places)
    arrays = [refs[2 * number : 2 * number + 2] for number in range(count)]
    outs, (scores, context) = refs[-2 - n_outs : -2], refs[-2:]
    slots, width = context.shape
    heads = width // HD
    wanted = rows_ref[...]
    head_of = lax.broadcasted_iota(jnp.int32, (slots, width), 1) // HD

    def positions(number):
        column = lax.broadcasted_iota(jnp.int32, (1, arrays[number][1].shape[0]), 1)
        position = column
        for start, _, first in places[number]:
            position = jnp.where(column >= first, column - first + start, position)
        return position

    query = None
    for number in range(origin):
        one_hot = (positions(number) == wanted).astype(f32).astype(bf16)
        part = jnp.dot(one_hot, arrays[number][0][...], preferred_element_type=f32)
        query = part if query is None else query + part
    stacked = stack_heads(query.astype(bf16), head_of, heads)
    top, starts = None, []
    for number in range(count):
        starts.append(starts[-1] + arrays[number - 1][1].shape[0] if number else 0)
        key = arrays[number][1][:, :width]
        far = positions(number) - wanted
        usable = (far <= RADIUS) & (far >= -RADIUS)
        if number >= origin:
            usable = usable & (ends[number - origin] > 0)
        piece = lax.dot_general(stacked, key, (((1,), (1,)), ((), ())), preferred_element_type=f32)
        piece = jnp.where(usable[None], piece.reshape(heads, slots, key.shape[0]), -jnp.inf)
        scores[:, :, starts[number] : starts[number] + key.shape[0]] = piece
        high = jnp.max(piece, axis=-1, keepdims=True)
        top = high if top is None else jnp.maximum(top, high)
    total, mixed = None, None
    for number in range(count):
        value = arrays[number][1][:, width:]
        expo = jnp.exp(scores[:, :, starts[number] : starts[number] + value.shape[0]] - top)
        amount = jnp.sum(expo, axis=-1, keepdims=True)
        expo = expo.astype(bf16).reshape(heads * slots, value.shape[0])
        part = jnp.dot(expo, value, preferred_element_type=f32)
        total = amount if total is None else total + amount
        mixed = part if mixed is None else mixed + part
    mixed = mixed.reshape(heads, slots, width) * (1.0 / total)
    context[...] = pick_heads(mixed, head_of)
    project(context, weight_ref, offsets, outs)


def routed_attention(places, arrays, ends, offsets, route_rows, attn_out, split, origin):
    slots = route_rows.shape[1]
    width, features = attn_out.shape
    flat = [piece for pair in arrays for piece in pair]
    outs = partial_shapes(split, slots, features, width)
    heads = width // HD
    span = sum(pair[1].shape[0] for pair in arrays)
    return pl.pallas_call(
        functools.partial(routed_kernel, places, len(outs), origin),
        out_shape=outs,
        in_specs=[SMEM, SMEM, VMEM, VMEM] + [VMEM] * len(flat),
        out_specs=[VMEM] * len(outs),
        scratch_shapes=[pltpu.VMEM((heads, slots, span), f32), pltpu.VMEM((slots, width), bf16)],
        compiler_params=params(20),
        cost_estimate=cost(2 * slots * (2 * span * width * heads + width * features)),
        name="routed_attention",
    )(ends, offsets, route_rows.reshape(slots, 1), attn_out, *flat)


def ffn_kernel(count, n_outs, tile, offsets, gain_ref, in_ref, down_hbm, *refs):
    blocks, outs = refs[:count], refs[-6 - n_outs : -6]
    normed, hidden, gate_ref, up_ref, down_ref, semaphores = refs[-6:]
    features, width = normed.shape[1], blocks[0].shape[1]
    tiles = [slice(start, start + tile) for start in range(0, hidden.shape[1], tile)]
    copies = []

    def start(source, target):
        copies.append(pltpu.make_async_copy(source, target, semaphores.at[len(copies)]))
        copies[-1].start()

    for columns in tiles:
        start(in_ref.at[0, :, columns], gate_ref.at[:, columns])
        start(in_ref.at[1, :, columns], up_ref.at[:, columns])
    if n_outs == 1:
        start(down_hbm, down_ref)
    else:
        for number in range(8):
            columns = pl.ds(pl.multiple_of(offsets[8 + number], width), width)
            start(down_hbm.at[:, columns], down_ref.at[:, number * width : (number + 1) * width])
    values = [block[...] for block in blocks]
    scale = row_scale(values, features)
    for number, value in enumerate(values):
        columns = columns_of(count, width, offsets, number)
        value = value.astype(f32) * scale * gain_ref[:, columns].astype(f32)
        normed[:, columns] = value.astype(bf16)
    for number, columns in enumerate(tiles):
        copies[2 * number].wait()
        gate = jnp.dot(normed[...], gate_ref[:, columns], preferred_element_type=f32)
        copies[2 * number + 1].wait()
        up = jnp.dot(normed[...], up_ref[:, columns], preferred_element_type=f32)
        hidden[:, columns] = (jax.nn.gelu(gate, approximate=True) * up).astype(bf16)
    if n_outs == 1:
        copies[-1].wait()
        outs[0][...] = jnp.dot(hidden[...], down_ref[...], preferred_element_type=f32).astype(bf16)
    else:
        for number in range(8):
            copies[2 * len(tiles) + number].wait()
            weight = down_ref[:, number * width : (number + 1) * width]
            value = jnp.dot(hidden[...], weight, preferred_element_type=f32)
            outs[number // 4][number % 4] = value.astype(bf16)


def ffn(blocks, offsets, gain_row, ffn_in, ffn_out, split, after):
    rows, width = blocks[0].shape
    hidden, features = ffn_out.shape
    count = len(blocks)
    tile = 512 if hidden % 512 == 0 else 128
    outs = partial_shapes(split, rows, features, width)
    return pl.pallas_call(
        functools.partial(ffn_kernel, count, len(outs), tile),
        out_shape=outs,
        in_specs=[SMEM, VMEM, ANY, ANY] + [VMEM] * count + [ANY] * len(after),
        out_specs=[VMEM] * len(outs),
        scratch_shapes=[
            pltpu.VMEM((rows, features), bf16),
            pltpu.VMEM((rows, hidden), bf16),
            pltpu.VMEM((features, hidden), bf16),
            pltpu.VMEM((features, hidden), bf16),
            pltpu.VMEM((hidden, features), bf16),
            pltpu.SemaphoreType.DMA((2 * hidden // tile + 8,)),
        ],
        compiler_params=params(38),
        cost_estimate=cost(2 * rows * features * 3 * hidden),
        name="heavy_ffn",
    )(
        offsets,
        gain_row,
        pltpu.with_memory_space_constraint(ffn_in, pltpu.HBM),
        pltpu.with_memory_space_constraint(ffn_out, pltpu.HBM),
        *blocks,
        *after,
    )


def total_of(refs):
    total = None
    for ref in refs:
        wide = (ref[...] if len(ref.shape) == 2 else ref[0]).astype(f32)
        total = wide if total is None else total + wide
    return total


def spread_kernel(groups, rows_ref, used_ref, *refs):
    pieces, terms, out_ref = refs[: len(groups)], refs[len(groups) : -1], refs[-1]
    slots = rows_ref.shape[1]
    heavy = jnp.where(used_ref[...] > 0, total_of(terms), 0.0)
    coarse = heavy.astype(bf16)
    fine = (heavy - coarse.astype(f32)).astype(bf16)
    for (start, rows), piece in zip(groups, pieces):
        position = lax.broadcasted_iota(jnp.int32, (rows, slots), 0) + start
        one_hot = (position == rows_ref[...]).astype(f32).astype(bf16)
        extra = jnp.dot(one_hot, coarse, preferred_element_type=f32)
        extra += jnp.dot(one_hot, fine, preferred_element_type=f32)
        out_ref[start : start + rows, :] = (piece[...].astype(f32) + extra).astype(bf16)


def spread(groups, pieces, terms, route_rows, usable_slots):
    rows, width = sum(rows for _, rows in groups), pieces[0].shape[1]
    return pl.pallas_call(
        functools.partial(spread_kernel, groups),
        out_shape=jax.ShapeDtypeStruct((rows, width), bf16),
        in_specs=[VMEM] * (2 + len(pieces) + len(terms)),
        out_specs=VMEM,
        compiler_params=params(12),
        name="spread_rows",
    )(route_rows, usable_slots.astype(jnp.int32)[:, None], *pieces, *terms)


def plan(total):
    middle = total // 2
    chunks = [[0, 1, total - 2, total - 1], list(range(2, middle)), list(range(middle, total - 2))]
    return chunks, [list(range(middle)), list(range(middle, total))]


def local(
    residual, attn_gain, attn_in, attn_out, ffn_gain, ffn_in, ffn_out, route_rows, route_counts
):
    seq_count = lax.axis_size("seq")
    seq_index = lax.axis_index("seq")
    tok_rows, width = residual.shape
    split = lax.axis_size("tp") == 8
    chunks, groups = plan(tok_rows // BLK)
    if split:
        pairs = Pairs()
        offsets = pairs.places(width)
        gather = functools.partial(gather_few, pairs)
        reduce = functools.partial(reduce_blocks, pairs)
        whole, late = gather_blocks(pairs, residual, chunks)
    else:
        offsets = jnp.zeros((1,), jnp.int32)

        def gather(own):
            return [lax.all_gather(own, "tp", axis=1, tiled=True)]

        def reduce(part):
            total = lax.psum_scatter(part, "tp", scatter_dimension=1, tiled=True)
            return [total], [total]

        whole, late = gather(residual), [[]] * len(chunks)

    ends = jnp.stack([seq_index > 0, seq_index < seq_count - 1]).astype(jnp.int32)
    keys, arrays, places = {}, [], []
    low = high = None
    for number, blocks in enumerate(chunks):
        after = [arrays[-1][0]] if arrays else []
        runs = runs_of(blocks)
        query, pair = qkv(whole + late[number], runs, offsets, attn_gain[None], attn_in, after)
        for at, block in enumerate(blocks):
            keys[block] = (len(arrays), at * BLK)
        arrays.append([query, pair])
        places.append(runs)
        if number == 0:
            up = [(i, i + 1) for i in range(seq_count - 1)]
            down = [(target, source) for source, target in up]
            low = lax.ppermute(pair[-BLK:], "seq", up)
            high = lax.ppermute(pair[:BLK], "seq", down)
    origin = len(arrays)
    keys["low"] = keys[-1] = (origin, 0)
    keys["high"] = keys[tok_rows // BLK] = (origin + 1, 0)
    arrays += [[low, low], [high, high]]
    places += [[(-BLK, BLK, 0)], [(tok_rows, BLK, 0)]]

    routed = routed_attention(places, arrays, ends, offsets, route_rows, attn_out, split, origin)
    mixed, _ = reduce(*routed)
    taken = (jnp.take(residual, route_rows[0], axis=0).astype(f32) + total(mixed)).astype(bf16)

    spans, pieces, previous, moves = [], [], routed[0], []
    for number, queries in enumerate(groups):
        needed = sorted({keys[b + step][0] for b in queries for step in (-1, 0, 1)})
        place = {array: at for at, array in enumerate(needed)}
        inner = {name: (place.get(array), start) for name, (array, start) in keys.items()}
        inner["low"] = inner[-1]
        inner["high"] = inner[tok_rows // BLK]
        used = [arrays[array] for array in needed]
        parts = attention(queries, inner, used, ends, offsets, attn_out, split, [previous])
        previous = parts[0]
        terms, moved = reduce(*parts)
        moves.append(moved)
        spans.append((queries[0] * BLK, len(queries) * BLK))
        pieces.append((rows_of(residual, queries).astype(f32) + total(terms)).astype(bf16))

    slots = jnp.arange(route_rows.shape[1], dtype=jnp.int32)
    row_count = lax.dynamic_index_in_dim(route_counts, seq_index, 0, keepdims=False)
    parts = ffn(gather(taken), offsets, ffn_gain[None], ffn_in, ffn_out, split, moves[0][1:2])
    terms, _ = reduce(*parts)
    return spread(spans, pieces, terms, route_rows, slots < row_count)


def solution(mesh):
    in_specs = (
        P("seq", "tp"),
        P(),
        P(None, None, "tp"),
        P("tp", None),
        P(),
        P(None, None, "tp"),
        P("tp", None),
        P("seq", None),
        P(),
    )
    out_specs = P("seq", "tp")
    return jax.shard_map(local, mesh=mesh, in_specs=in_specs, out_specs=out_specs, check_vma=False)
```
